256 devices in a mesh: seq: 32 (over z, y_hi, core), dp: 8 (over x, y_lo).
Axes of the slice: x: 4, y: 4 (y_hi: 2, y_lo: 2; y = y_hi * 2 + y_lo), z: 8, core: 2. Of those that a mesh axis runs over, the one named last changes fastest.
Arguments:
- queries: bfloat16 [8, 4096, 3072], P('dp', 'seq'), may hold values from -9 to 9
- keys: bfloat16 [8, 4096, 512], P('dp', 'seq'), may hold values from -6 to 6
- values: bfloat16 [8, 4096, 512], P('dp', 'seq'), may hold values from -6 to 6
- stretch_ids: int32 [8, 4096], P('dp'), may hold values from 0 to 63, never falling along the last dimension, each value on 1 to 256 neighbouring positions
- residual_in: bfloat16 [8, 4096, 6144], P(None, 'seq', 'dp'), may hold values from -6 to 6
- out_proj: bfloat16 [3072, 6144], P(None, 'dp'), may hold values from -0.875 to 0.875
- proj_in: bfloat16 [6144, 1024], P('dp'), may hold values from -0.078125 to 0.078125
- proj_out: bfloat16 [1024, 1536], replicated, may hold values from -0.1875 to 0.1875
- teacher_store: bfloat16 [8, 32, 256, 1536], P('dp', 'seq'), may hold values from -6 to 6
- reader_map: int32 [8, 4096, 1], P('dp', 'seq'), may hold values from 0 to 31; in each aligned block of 128 rows (0 to 127, 128 to 255, ..., all dimensions but the last counted through in order) at most 8 rows name the same one
Outputs:
- alignment: float32 [8, 4096], P('dp', 'seq')
- grad_proj_out: float32 [1024, 1536], P(('seq', 'dp'))
The draws below stay inside these ranges and needn't reach their ends.
Inputs may be any that keep to these rules, and one draw needn't show every extreme that they name: `stretch_ids`: along each clip the stretch number never falls; each stretch holds 1 to 256 tokens and some stretch holds exactly 256. `reader_map`: within each aligned block of 128 tokens (the tokens of one device) no reader is named more than 8 times, a bound that some block reaches; every reader is named somewhere.
All inputs are finite; a program needn't handle non-finite values.
Results may differ from the reference program's by a relative error of at most 0.024.
Values may be sent and summed in bfloat16 or wider, within the bound.
No kernel may reach another device: no remote copies, remote signals or barrier semaphores. Data moves between devices by JAX's collectives and lax.ppermute only.
A program may use at most 128 MiB of HBM per device.

```python
import math
import jax
import jax.numpy as jnp
import numpy as np
from jax import lax

D = 6144
HD = 128
HEADS = 24
GROUPS = 4
PH = 1024
TD = 1536
TOK_DEV = 128
CLIPS = 8
SEQLEN = 4096
STRETCH_MOST = 256
CAP = 8
N_SEQ = 32


def shared_keys(key):
    base = jax.random.normal(key, (CLIPS, SEQLEN, GROUPS * HD), jnp.float32)
    return jnp.clip(base, -6.0, 6.0)


def draw_keys(key, part):
    base = shared_keys(key)
    return base.astype(jnp.bfloat16)


def draw_queries(key, part):
    key = jax.random.fold_in(key, 5)
    fresh = jnp.clip(jax.random.normal(key, (CLIPS, SEQLEN, HEADS * HD), jnp.float32), -6.0, 6.0)
    return fresh.astype(jnp.bfloat16)


def steps_of(key, shape, cuts, smallest, high):
    gain = 1.0
    for dim, blocks in cuts:
        steps = jax.random.uniform(jax.random.fold_in(jax.random.fold_in(key, 6), dim), (blocks,), jnp.float32, smallest / len(cuts), high / len(cuts))
        gain = gain * jnp.repeat(jnp.exp(steps), shape[dim] // blocks).reshape((-1,) + (1,) * (len(shape) - 1 - dim))
    return gain


def profile(amount, total, bound, slope):
    loads = [(1 << 20) // math.isqrt(standing ** slope) + 1 for standing in range(2, amount + 1)]
    spare, counts = total - bound - (amount - 1), [1] * (amount - 1)
    while spare > 0:
        movable = [i for i in range(amount - 1) if counts[i] < bound]
        mass, remaining = sum([loads[i] for i in movable]), spare
        for i in movable:
            extra = min(bound - counts[i], max(1, remaining * loads[i] // mass), spare)
            counts[i] = counts[i] + extra
            spare = spare - extra
    return np.array([bound] + counts)


def uneven(stream_key, amount, total, most, slope):
    if amount == 2:
        one = jax.random.randint(stream_key, (), max(1, total - most), min(most, total - 1) + 1)
        return jnp.stack([one, total - one])
    lengths = jnp.asarray(profile(amount, total, most, slope), jnp.int32)
    couples = (amount - 1) // 2
    source_of, receiver = lengths[1:1 + 2 * couples:2], lengths[2:2 + 2 * couples:2]
    margin = jnp.minimum(source_of - 1, most - receiver)
    shifted = jax.random.randint(jax.random.fold_in(stream_key, 1), (couples,), 0, 1 << 20) % (margin + 1)
    lengths = lengths.at[1:1 + 2 * couples:2].set(source_of - shifted).at[2:2 + 2 * couples:2].set(receiver + shifted)
    return lengths[jax.random.permutation(jax.random.fold_in(stream_key, 2), amount)]


def routed_block(own_key, own, number, rows, amount, top, reach, skew):
    ranking = jax.random.permutation(own_key, amount)
    crowded, ordinary = shares(amount, rows * top, reach, skew, True), shares(amount, rows * top, reach, skew, False)
    places = jnp.arange(amount)

    def named(lengths, rotation):
        used = int((lengths > 0).sum())
        fixed = max(1, used // 4)
        shifted = fixed + (places - fixed + rotation * (used - fixed)) % max(1, amount - fixed)
        return jnp.zeros((amount,), jnp.int32).at[ranking[jnp.where(places < fixed, places, shifted)]].set(jnp.asarray(lengths, jnp.int32))

    lengths = jnp.where(number % 4 == 0, named(crowded, number // 4), named(ordinary, number - number // 4 - 1))
    mixed = jax.random.permutation(jax.random.fold_in(own, 3), amount)
    giver, sink = mixed[0:amount // 2 * 2:2], mixed[1:amount // 2 * 2:2]
    margin = jnp.minimum(lengths[giver] - 1, reach - lengths[sink]) // 2
    margin = jnp.where((giver == ranking[0]) | (sink == ranking[0]) | (lengths[sink] == 0), 0, jnp.maximum(margin, 0))
    shifted = jax.random.randint(jax.random.fold_in(own, 4), (amount // 2,), 0, 1 << 20) % (margin + 1)
    lengths = lengths.at[giver].add(-shifted).at[sink].add(shifted)
    items = jnp.searchsorted(jnp.cumsum(lengths), jnp.arange(rows * top), side="right").astype(jnp.int32)
    grid = items.reshape(top, rows).T
    grid = grid[jax.random.permutation(jax.random.fold_in(own, 1), rows)]
    rotation = jax.random.randint(jax.random.fold_in(own, 2), (rows, 1), 0, top)
    return jnp.take_along_axis(grid, (jnp.arange(top)[None, :] + rotation) % top, axis=1)


def shares(amount, total, bound, slope, full):
    weights = [(1 << 20) // math.isqrt(standing ** slope) + 1 for standing in range(1, amount + 1)]
    largest = bound if full else min(bound, max(-(-total // amount), total * weights[0] // sum(weights)))
    least = 1 if total - largest >= amount - 1 else 0
    holding, spare = [largest] + [least] * (amount - 1), total - largest - least * (amount - 1)
    while spare > 0:
        free = [i for i in range(1, amount) if holding[i] < largest] or [i for i in range(1, amount) if holding[i] < bound]
        mass, remaining = sum([weights[i] for i in free]), spare
        for i in free:
            more = min(bound - holding[i], max(1, remaining * weights[i] // mass), spare)
            holding[i] = holding[i] + more
            spare = spare - more
    return np.array(holding)


def normal_values(key, shape, deviation, limit, cuts=(), kind=jnp.bfloat16):
    drawn = jax.random.normal(key, shape, jnp.float32) * deviation
    if len(cuts) > 0:
        drawn = steps_of(key, shape, cuts, -0.22, 0.18) * drawn
    return jnp.clip(drawn, min=-limit, max=limit).astype(kind)


def setup_inputs(seed: int = 0) -> dict:
    key_of = jax.random.split(jax.random.key(seed), 11)
    queries = draw_queries(jax.random.fold_in(key_of[10], 71), 0)
    keys = draw_keys(jax.random.fold_in(key_of[10], 71), 0)
    values = normal_values(key_of[2], (CLIPS, SEQLEN, GROUPS * HD), 1.0, 6.0, ((0, 8), (1, 32)))
    stretch_ids = jax.vmap(lambda own: jnp.searchsorted(jnp.cumsum(uneven(own, 2 * N_SEQ, SEQLEN, STRETCH_MOST, 1)), jnp.arange(SEQLEN), side="right"))(jax.random.split(key_of[3], CLIPS)).reshape((CLIPS, SEQLEN)).astype(jnp.int32)
    residual_in = normal_values(key_of[4], (CLIPS, SEQLEN, D), 0.5, 6.0, ((1, 32), (2, 8)))
    out_proj = normal_values(key_of[5], (HEADS * HD, D), (max(1, HEADS * HD // 64)) ** -0.5, 0.875, ((1, 8),))
    proj_in = normal_values(key_of[6], (D, PH), D ** -0.5, 0.078125, ((0, 8),))
    proj_out = normal_values(key_of[7], (PH, TD), PH ** -0.5, 0.1875)
    teacher_store = normal_values(key_of[8], (CLIPS, N_SEQ, N_SEQ * CAP, TD), 1.0, 6.0, ((0, 8), (1, 32)))
    reader_map_keys = jax.random.split(jax.random.fold_in(key_of[9], 1), CLIPS * SEQLEN // TOK_DEV)
    reader_map_turns = jax.random.permutation(jax.random.fold_in(key_of[9], 3), CLIPS * SEQLEN // TOK_DEV)
    reader_map = jax.vmap(lambda own, number: routed_block(jax.random.fold_in(key_of[9], 2), own, number, TOK_DEV, N_SEQ, 1, CAP, 2))(reader_map_keys, reader_map_turns).reshape((CLIPS, SEQLEN, 1))
    return {"queries": queries, "keys": keys, "values": values, "stretch_ids": stretch_ids, "residual_in": residual_in, "out_proj": out_proj, "proj_in": proj_in, "proj_out": proj_out, "teacher_store": teacher_store, "reader_map": reader_map}


NEG = -1e+30
EPS = 1e-06

def attend_clip(query_rows, key_rows, value_rows, stretch_row):
    per_group = HEADS // GROUPS
    span = 512 if SEQLEN % 512 == 0 else SEQLEN
    key_heads = key_rows.reshape(SEQLEN, GROUPS, HD).astype(jnp.float32)
    value_heads = value_rows.reshape(SEQLEN, GROUPS, HD).astype(jnp.float32)
    query_blocks = query_rows.reshape(SEQLEN // span, span, GROUPS, per_group, HD)
    stretch_blocks = stretch_row.reshape(SEQLEN // span, span)

    def one_block(pieces):
        query_part, stretch_part = pieces
        scores = jnp.einsum('tgrd,pgd->tgrp', query_part.astype(jnp.float32), key_heads) * HD ** (-0.5)
        visible = stretch_row[None, :] <= stretch_part[:, None]
        scores = jnp.where(visible[:, None, None, :], scores, NEG)
        highest = lax.optimization_barrier(jnp.max(scores, axis=-1, keepdims=True))
        weights = jnp.exp(scores - highest)
        rounded = lax.optimization_barrier(weights.astype(jnp.bfloat16)).astype(jnp.float32)
        numer = jnp.einsum('tgrp,pgd->tgrd', rounded, value_heads)
        return (numer / lax.optimization_barrier(jnp.sum(weights, axis=-1))[..., None]).astype(jnp.bfloat16)
    result = lax.map(one_block, (query_blocks, stretch_blocks))
    return result.reshape(SEQLEN, HEADS * HD)

def teacher_clip(store, routes):
    readers = routes[:, 0].reshape(N_SEQ, TOK_DEV)
    onehot = (readers[:, :, None] == jnp.arange(N_SEQ, dtype=jnp.int32)[None, None, :]).astype(jnp.int32)
    before = jnp.cumsum(onehot, axis=1) - onehot
    rank = lax.optimization_barrier(jnp.sum(before * onehot, axis=2))
    owner = jnp.arange(N_SEQ, dtype=jnp.int32)[:, None]
    flat = (readers * (N_SEQ * CAP) + owner * CAP + rank).astype(jnp.int32)
    rows = store.reshape(N_SEQ * N_SEQ * CAP, TD)
    return jnp.take(rows, flat.reshape(SEQLEN), axis=0)

def align(projected, target):
    target = target.astype(jnp.float32)
    proj_square = lax.optimization_barrier(jnp.sum(projected * projected, axis=-1)) + EPS
    target_square = lax.optimization_barrier(jnp.sum(target * target, axis=-1)) + EPS
    inner = lax.optimization_barrier(jnp.sum(projected * target, axis=-1))
    denominator = jnp.sqrt(proj_square * target_square)
    cosine = inner / denominator
    grad_rows = -(target / denominator[:, None] - (cosine / proj_square)[:, None] * projected)
    return (cosine, grad_rows)

def reference(queries, keys, values, stretch_ids, residual_in, out_proj, proj_in, proj_out, teacher_store, reader_map):

    def per_clip(pieces):
        query_rows, key_rows, value_rows, stretch_row, residual, store, routes = pieces
        attended = attend_clip(query_rows, key_rows, value_rows, stretch_row)
        hidden = (residual.astype(jnp.float32) + jnp.dot(attended, out_proj, preferred_element_type=jnp.float32)).astype(jnp.bfloat16)
        pre = jnp.dot(hidden, proj_in, preferred_element_type=jnp.float32)
        act = jax.nn.silu(pre).astype(jnp.bfloat16)
        projected = jnp.dot(act, proj_out, preferred_element_type=jnp.float32)
        target = teacher_clip(store, routes)
        cosine, grad_rows = align(projected, target)
        grad = jnp.dot(act.T, grad_rows.astype(jnp.bfloat16), preferred_element_type=jnp.float32)
        return (cosine, grad)
    cosines, grads = lax.map(per_clip, (queries, keys, values, stretch_ids, residual_in, teacher_store, reader_map))
    return (cosines, lax.optimization_barrier(jnp.sum(grads, axis=0)))
```

```python
import functools

import jax
import jax.numpy as jnp
from jax import lax
from jax.experimental import pallas as pl
from jax.experimental.pallas import tpu as pltpu
from jax.sharding import Mesh, PartitionSpec as P

HD = 128
HEADS = 24
GROUPS = 4
PER = HEADS // GROUPS
NEG = -1e30
EPS = 1e-06
SCALE2 = HD ** (-0.5) * 1.4426950408889634

AXES = ("z", "yh", "core", "x", "yl")
SIZES = (8, 2, 2, 4, 2)
SEQ = ("z", "yh", "core")
DP = ("x", "yl")
QUAD = ("yh", "core")


def flash_kernel(n, first, last, meta, q_ref, c_ref, *refs):
    kv = refs[:n]
    refs = refs[n:]
    if not first:
        m_in, l_in, a_in = refs[:3]
        refs = refs[3:]
    if last:
        out, m_ref, l_ref, a_ref = refs[:4]
        vt = refs[4:]
    else:
        m_ref, l_ref, a_ref = refs[:3]
        vt = refs[3:]

    @pl.when(pl.program_id(0) == 0)
    def _():
        for j in range(n):
            vt[j][...] = kv[j][:, HD:].T

    if first:
        m_ref[...] = jnp.full(m_ref.shape, NEG, jnp.float32)
        l_ref[...] = jnp.zeros(l_ref.shape, jnp.float32)
        a_ref[...] = jnp.zeros(a_ref.shape, jnp.float32)
    else:
        m_ref[...] = m_in[...]
        l_ref[...] = l_in[...]
        a_ref[...] = a_in[...]
    lowest = meta[n]
    highest = meta[n + 1]
    for j in range(n):
        base = meta[j]
        rows = kv[j].shape[0]

        def step(masked, j=j, base=base, rows=rows):
            s = jnp.dot(kv[j][:, :HD], q_ref[...], preferred_element_type=jnp.float32)
            if masked:
                place = lax.broadcasted_iota(jnp.int32, s.shape, 0)
                s = jnp.where(place < c_ref[...] - base, s, NEG)
            old = m_ref[0]
            new = jnp.maximum(old, jnp.max(s, axis=0, keepdims=True))
            p = jnp.exp2((s - new) * SCALE2)
            factor = jnp.exp2((old - new) * SCALE2)
            m_ref[0] = new
            l_ref[0] = l_ref[0] * factor + jnp.sum(p, axis=0, keepdims=True)
            a_ref[...] = a_ref[...] * factor + jnp.dot(
                vt[j][...], p.astype(jnp.bfloat16), preferred_element_type=jnp.float32
            )

        whole = base + rows <= lowest

        @pl.when(whole)
        def _(step=step):
            step(False)

        @pl.when(jnp.logical_and(jnp.logical_not(whole), base < highest))
        def _(step=step):
            step(True)

    if last:
        out[...] = (a_ref[...] / l_ref[0]).astype(out.dtype)


def flash(q_t, counts, bounds, pieces, bases, state, last):
    n = len(pieces)
    tokens = q_t.shape[1]
    first = state is None
    meta = jnp.concatenate([jnp.stack(bases).astype(jnp.int32), bounds])
    row = pl.BlockSpec((1, 1, tokens), lambda h, meta: (h, 0, 0))
    head = pl.BlockSpec((HD, tokens), lambda h, meta: (h, 0))
    f32 = jnp.float32
    in_specs = [head, pl.BlockSpec((1, tokens), lambda h, meta: (0, 0))]
    in_specs += [pl.BlockSpec(p.shape, lambda h, meta: (0, 0)) for p in pieces]
    args = [q_t, counts] + list(pieces)
    if not first:
        in_specs += [row, row, head]
        args += list(state)
    scratch = [pltpu.VMEM((HD, p.shape[0]), jnp.bfloat16) for p in pieces]
    if last:
        out_specs = head
        out_shape = jax.ShapeDtypeStruct((PER * HD, tokens), jnp.bfloat16)
        scratch = [
            pltpu.VMEM((1, 1, tokens), f32),
            pltpu.VMEM((1, 1, tokens), f32),
            pltpu.VMEM((HD, tokens), f32),
        ] + scratch
    else:
        out_specs = [row, row, head]
        out_shape = [
            jax.ShapeDtypeStruct((PER, 1, tokens), f32),
            jax.ShapeDtypeStruct((PER, 1, tokens), f32),
            jax.ShapeDtypeStruct((PER * HD, tokens), f32),
        ]
    keys = sum(p.shape[0] for p in pieces)
    return pl.pallas_call(
        functools.partial(flash_kernel, n, first, last),
        grid_spec=pltpu.PrefetchScalarGridSpec(
            num_scalar_prefetch=1,
            grid=(PER,),
            in_specs=in_specs,
            out_specs=out_specs,
            scratch_shapes=scratch,
        ),
        out_shape=out_shape,
        compiler_params=pltpu.CompilerParams(vmem_limit_bytes=32 * 1024 * 1024),
        cost_estimate=pl.CostEstimate(
            flops=4 * PER * tokens * keys * HD,
            bytes_accessed=6 * PER * HD * tokens,
            transcendentals=PER * tokens * keys,
        ),
    )(meta, *args)


def shift(v, k):
    return lax.ppermute(v, "z", [(i, (i + k) % 8) for i in range(8)])


def align(projected, target):
    proj_square = jnp.sum(projected * projected, axis=-1) + EPS
    target_square = jnp.sum(target * target, axis=-1) + EPS
    inner = jnp.sum(projected * target, axis=-1)
    denominator = jnp.sqrt(proj_square * target_square)
    cosine = inner / denominator
    grad_rows = -(target / denominator[:, None] - (cosine / proj_square)[:, None] * projected)
    return (cosine, grad_rows)


def on_device(
    queries,
    keys,
    values,
    stretch_ids,
    residual_in,
    out_proj,
    proj_in,
    proj_out,
    teacher_store,
    reader_map,
):
    f32, bf16 = jnp.float32, jnp.bfloat16
    z = lax.axis_index("z")
    group = lax.axis_index(QUAD)
    core = lax.axis_index("core")
    rows = queries.shape[1]
    tokens = rows * 4

    kv = jnp.concatenate([keys[0].reshape(rows, GROUPS, HD), values[0].reshape(rows, GROUPS, HD)], axis=-1)
    kv = lax.all_to_all(kv.transpose(1, 0, 2), QUAD, 0, 0, tiled=True).reshape(tokens, 2 * HD)
    q = queries[0].reshape(rows, GROUPS, PER * HD).transpose(1, 0, 2)
    q = lax.all_to_all(q, QUAD, 0, 0, tiled=True).reshape(tokens, PER * HD)
    q_t = q.T

    wide = PER * HD // 8
    wo = lax.dynamic_slice_in_dim(out_proj, group * PER * HD + z * wide, wide)
    w = jnp.dot(wo, proj_in, preferred_element_type=f32).astype(bf16)
    w = lax.all_to_all(w.reshape(wide, 8, HD).transpose(1, 0, 2), DP, 0, 0, tiled=True)
    w = jnp.sum(w.astype(f32), axis=0).astype(bf16)
    w = lax.all_gather(w, "z", axis=0, tiled=True)
    w = lax.all_gather(w, DP, axis=0, tiled=False)

    clips = residual_in.shape[0]
    res = jnp.dot(
        residual_in.reshape(clips * rows, residual_in.shape[2]), proj_in, preferred_element_type=f32
    ).astype(bf16)
    res = lax.all_to_all(res.reshape(clips, rows, res.shape[1]), DP, 0, 0, tiled=True)
    res = jnp.sum(res.astype(f32), axis=0)

    store = teacher_store.reshape(32, 8, teacher_store.shape[3])
    arrived = lax.all_to_all(store, SEQ, 0, 0, tiled=True).reshape(256, store.shape[2])
    readers = reader_map[0, :, 0]
    onehot = (readers[:, None] == jnp.arange(32, dtype=jnp.int32)[None, :]).astype(jnp.int32)
    before = jnp.cumsum(onehot, axis=0) - onehot
    rank = jnp.sum(before * onehot, axis=1)
    pick = (readers * 8 + rank)[:, None] == jnp.arange(256, dtype=jnp.int32)[None, :]
    target = jnp.dot(pick.astype(bf16), arrived, preferred_element_type=f32)

    stretch = stretch_ids[0]
    mine = lax.dynamic_slice_in_dim(stretch, z * tokens, tokens)
    counts = jnp.sum((stretch[:, None] <= mine[None, :]).astype(jnp.int32), axis=0)
    bounds = jnp.stack([counts[0], counts[-1]])
    counts = counts[None, :]

    def base(k):
        return lax.rem(z + k + 8, 8) * tokens

    state = flash(q_t, counts, bounds, [kv], [base(0)], None, False)
    fore = back = kv
    for s in range(1, 4):
        fore, back = shift(fore, 1), shift(back, -1)
        state = flash(q_t, counts, bounds, [fore, back], [base(-s), base(s)], state, False)
    half = tokens // 2
    fore, back = shift(fore[:half], 1), shift(back[half:], -1)
    att = flash(q_t, counts, bounds, [fore, back], [base(4), base(4) + half], state, True)

    part = lax.dot_general(att, w, (((0,), (1,)), ((), ())), preferred_element_type=f32)
    part = part.reshape(4, rows, 8 * HD).astype(bf16)
    part = lax.all_to_all(part, QUAD, 0, 0, tiled=True)
    pre = jnp.sum(part.astype(f32), axis=0) + res
    act = jax.nn.silu(pre).astype(bf16)
    projected = jnp.dot(act, proj_out, preferred_element_type=f32)
    cosine, grad_rows = align(projected, target)
    delta = grad_rows.astype(bf16)

    at = jnp.arange(512, dtype=jnp.int32)
    column = (
        (at // 4 % 8) * 128 + (at // 256) * 64 + (at // 64 % 4) * 8 + (at // 32 % 2) * 4 + at % 4
    )

    def chosen(c):
        take = (column + c * 32)[:, None] == jnp.arange(1024, dtype=jnp.int32)[None, :]
        return lax.dot_general(
            take.astype(bf16), act, (((1,), (1,)), ((), ())), preferred_element_type=f32
        ).astype(bf16)

    swap = [(0, 1), (1, 0)]
    other_act = lax.ppermute(chosen(1 - core), "core", swap)
    other_delta = lax.ppermute(delta, "core", swap)
    grads = jnp.dot(chosen(core), delta, preferred_element_type=f32) + jnp.dot(
        other_act, other_delta, preferred_element_type=f32
    )
    grads = grads.astype(bf16).reshape(16, 32, grads.shape[1])
    grads = lax.all_to_all(grads, ("yh", "x", "yl"), 0, 0, tiled=True)
    grads = jnp.sum(grads.astype(f32), axis=0).reshape(8, 4, grads.shape[2])
    grads = jnp.sum(lax.all_to_all(grads, "z", 0, 0, tiled=True), axis=0)
    return (cosine.reshape(1, rows), grads)


def solution(mesh):
    fine = Mesh(mesh.devices.reshape(SIZES), AXES)
    return jax.shard_map(
        on_device,
        mesh=fine,
        in_specs=(
            P(DP, SEQ, None),
            P(DP, SEQ, None),
            P(DP, SEQ, None),
            P(DP, None),
            P(None, SEQ, DP),
            P(None, DP),
            P(DP, None),
            P(),
            P(DP, SEQ, None, None),
            P(DP, SEQ, None),
        ),
        out_specs=(P(DP, SEQ), P(SEQ + DP, None)),
        check_vma=False,
    )
```

```python
import functools

import jax
import jax.numpy as jnp
from jax import lax
from jax.experimental import pallas as pl
from jax.experimental.pallas import tpu as pltpu
from jax.sharding import Mesh, PartitionSpec as P

HD = 128
HEADS = 24
GROUPS = 4
PER = HEADS // GROUPS
HEADS_STEP = 3
NEG = -1e30
EPS = 1e-06
SCALE2 = HD ** (-0.5) * 1.4426950408889634

AXES = ("z", "yh", "core", "x", "yl")
SIZES = (8, 2, 2, 4, 2)
SEQ = ("z", "yh", "core")
DP = ("x", "yl")
QUAD = ("yh", "core")
SWAP = ((0, 1), (1, 0))
NEAR = ((0, 1), (1, 0), (2, 3), (3, 2))
FAR = ((0, 3), (3, 0), (1, 2), (2, 1))


def flash_kernel(cuts, shifts, first, last, meta, *refs):
    if first:
        parts, refs = refs[:4], refs[4:]
    else:
        q_ref, refs = refs[0], refs[1:]
    n = len(cuts)
    c_ref, kv, refs = refs[0], refs[1 : 1 + n], refs[1 + n :]
    if not first:
        m_in, l_in, a_in = refs[:3]
        refs = refs[3:]
    if last:
        out, m_ref, l_ref, a_ref, qq, kk, vt = refs
    else:
        m_ref, l_ref, a_ref = refs[:3]
        qq, kk, vt = refs[-3:]
        if first:
            q_ref = refs[3]
    chunks = kk.shape[0]
    tokens = kk.shape[1]

    @pl.when(pl.program_id(0) == 0)
    def _():
        for piece, (j, row) in zip(kv, cuts):
            span = slice(row, row + piece.shape[0])
            kk[j, span, :HD] = piece[:, :HD]
            kk[j, span, HD:] = piece[:, :HD]
            vt[j, :HD, span] = piece[:, HD:].T
        vt[:, HD:, :] = jnp.ones((chunks, vt.shape[1] - HD, tokens), vt.dtype)

    if first:
        for i, part in enumerate(parts):
            rows = part.shape[0]
            for h in range(HEADS_STEP):
                q_ref[0, :, h * tokens + i * rows : h * tokens + (i + 1) * rows] = part[:, h * HD : (h + 1) * HD].T
        m_ref[...] = jnp.full(m_ref.shape, NEG, jnp.float32)
        l_ref[...] = jnp.zeros(l_ref.shape, jnp.float32)
        a_ref[...] = jnp.zeros(a_ref.shape, jnp.float32)
    else:
        m_ref[...] = m_in[...]
        l_ref[...] = l_in[...]
        a_ref[...] = a_in[...]
    scaled = q_ref[0].astype(jnp.float32) * SCALE2
    high = scaled.astype(jnp.bfloat16)
    qq[:HD] = high
    qq[HD:] = (scaled - high.astype(jnp.float32)).astype(jnp.bfloat16)

    def chunk(j, carry):
        far = shifts[0]
        for i in range(1, chunks):
            far = jnp.where(j == i, shifts[i], far)
        base = lax.rem(meta[0] + far, 8) * tokens

        def step(masked):
            s = jnp.dot(kk[j], qq[...], preferred_element_type=jnp.float32)
            if masked:
                place = lax.broadcasted_iota(jnp.int32, s.shape, 0) ^ meta[3]
                s = jnp.where(place < c_ref[...] - base, s, NEG)
            old = m_ref[0]
            new = jnp.maximum(old, jnp.max(s, axis=0, keepdims=True))
            p = jnp.exp2(s - new).astype(jnp.bfloat16)
            factor = jnp.exp2(old - new)
            sums = jnp.dot(vt[j], p, preferred_element_type=jnp.float32)
            m_ref[0] = new
            l_ref[0] = l_ref[0] * factor + sums[HD : HD + 1]
            a_ref[0] = a_ref[0] * factor + sums[:HD]

        whole = base + tokens <= meta[1]

        @pl.when(whole)
        def _():
            step(False)

        @pl.when(jnp.logical_and(jnp.logical_not(whole), base < meta[2]))
        def _():
            step(True)

        return carry

    lax.fori_loop(0, chunks, chunk, 0)
    if last:
        done = (a_ref[0] / l_ref[0]).astype(out.dtype)
        rows = tokens // 4
        for h in range(HEADS_STEP):
            for to, block in enumerate((1, 3, 0, 2)):
                start = h * tokens + block * rows
                out[to * rows : (to + 1) * rows, h * HD : (h + 1) * HD] = done[:, start : start + rows].T


def flash(q_t, counts, meta, pieces, cuts, shifts, state, last):
    first = state is None
    tokens = counts.shape[1]
    wide = HEADS_STEP * tokens
    steps = PER // HEADS_STEP
    chunks = len(shifts)
    f32, bf16 = jnp.float32, jnp.bfloat16
    row = pl.BlockSpec((1, 1, wide), lambda h, meta: (h, 0, 0))
    head = pl.BlockSpec((1, HD, wide), lambda h, meta: (h, 0, 0))
    if first:
        in_specs = [pl.BlockSpec((tokens // 4, HEADS_STEP * HD), lambda h, meta: (0, h))] * 4
        args = list(q_t)
    else:
        in_specs = [head]
        args = [q_t]
    in_specs += [pl.BlockSpec((1, wide), lambda h, meta: (0, 0))]
    in_specs += [pl.BlockSpec(p.shape, lambda h, meta: (0, 0)) for p in pieces]
    args += [jnp.concatenate([counts] * HEADS_STEP, axis=1)] + list(pieces)
    if not first:
        in_specs += [row, row, head]
        args += list(state)
    scratch = [
        pltpu.VMEM((2 * HD, wide), bf16),
        pltpu.VMEM((chunks, tokens, 2 * HD), bf16),
        pltpu.VMEM((chunks, HD + 16, tokens), bf16),
    ]
    if last:
        out_specs = pl.BlockSpec((tokens, HEADS_STEP * HD), lambda h, meta: (0, h))
        out_shape = jax.ShapeDtypeStruct((tokens, PER * HD), bf16)
        scratch = [
            pltpu.VMEM((1, 1, wide), f32),
            pltpu.VMEM((1, 1, wide), f32),
            pltpu.VMEM((1, HD, wide), f32),
        ] + scratch
    else:
        out_specs = [row, row, head]
        out_shape = [
            jax.ShapeDtypeStruct((steps, 1, wide), f32),
            jax.ShapeDtypeStruct((steps, 1, wide), f32),
            jax.ShapeDtypeStruct((steps, HD, wide), f32),
        ]
        if first:
            out_specs.append(head)
            out_shape.append(jax.ShapeDtypeStruct((steps, HD, wide), bf16))
    return pl.pallas_call(
        functools.partial(flash_kernel, tuple(cuts), tuple(shifts), first, last),
        grid_spec=pltpu.PrefetchScalarGridSpec(
            num_scalar_prefetch=1,
            grid=(steps,),
            in_specs=in_specs,
            out_specs=out_specs,
            scratch_shapes=scratch,
        ),
        out_shape=out_shape,
        compiler_params=pltpu.CompilerParams(vmem_limit_bytes=48 * 1024 * 1024),
        cost_estimate=pl.CostEstimate(
            flops=40 * PER * tokens * tokens * chunks * HD,
            bytes_accessed=10 * PER * HD * tokens,
            transcendentals=PER * tokens * tokens * chunks,
        ),
    )(meta, *args)


def prepare_kernel(
    meta, q_ref, k_ref, v_ref, kv_own, kv_swap, kv_across, kv_both, q_own, q_swap, q_across, q_both
):
    width = PER * HD

    def take(g, kv, q):
        k = k_ref[:, pl.ds(pl.multiple_of(g * HD, HD), HD)]
        v = v_ref[:, pl.ds(pl.multiple_of(g * HD, HD), HD)]
        kv[...] = jnp.concatenate([k, v], axis=1)
        q[...] = q_ref[:, pl.ds(pl.multiple_of(g * width, HD), width)]

    group = meta[0]
    take(group, kv_own, q_own)
    take(group ^ 1, kv_swap, q_swap)
    take(group ^ 2, kv_across, q_across)
    take(group ^ 3, kv_both, q_both)


def prepare(queries, keys, values, group):
    rows = queries.shape[0]
    shapes = [(rows, w) for w in (2 * HD, PER * HD) for _ in range(4)]
    return pl.pallas_call(
        prepare_kernel,
        grid=(1,),
        in_specs=[pl.BlockSpec(memory_space=pltpu.SMEM)]
        + [pl.BlockSpec(a.shape, lambda i: (0, 0)) for a in (queries, keys, values)],
        out_specs=[pl.BlockSpec(s, lambda i: (0, 0)) for s in shapes],
        out_shape=[jax.ShapeDtypeStruct(s, jnp.bfloat16) for s in shapes],
        compiler_params=pltpu.CompilerParams(vmem_limit_bytes=60 * 1024 * 1024),
    )(group[None].astype(jnp.int32), queries, keys, values)


def shift(v, k):
    return lax.ppermute(v, "z", [(i, (i + k) % 8) for i in range(8)])


def hop_y(v, k):
    return lax.ppermute(v, ("yh", "yl"), [(i, (i + k) % 4) for i in range(4)])


def relay(v, k):
    return hop_y(hop_y(v, k), k)


def butterfly(v, axis, pairs):
    return (v.astype(jnp.float32) + lax.ppermute(v, axis, pairs).astype(jnp.float32)).astype(v.dtype)


def quad(v, k):
    return lax.ppermute(v, QUAD, [(i, i ^ k) for i in range(4)])


def after(v, other):
    return lax.optimization_barrier((v, other))[0]


def align(projected, target):
    proj_square = jnp.sum(projected * projected, axis=-1) + EPS
    target_square = jnp.sum(target * target, axis=-1) + EPS
    inner = jnp.sum(projected * target, axis=-1)
    denominator = jnp.sqrt(proj_square * target_square)
    cosine = inner / denominator
    grad_rows = -(target / denominator[:, None] - (cosine / proj_square)[:, None] * projected)
    return (cosine, grad_rows)


def on_device(
    queries,
    keys,
    values,
    stretch_ids,
    residual_in,
    out_proj,
    proj_in,
    proj_out,
    teacher_store,
    reader_map,
):
    f32, bf16 = jnp.float32, jnp.bfloat16
    z = lax.axis_index("z")
    yh = lax.axis_index("yh")
    core = lax.axis_index("core")
    group = yh * 2 + core
    rows = queries.shape[1]
    tokens = rows * 4
    width = PER * HD

    store = teacher_store.reshape(8, 4, 8, teacher_store.shape[3])
    store = lax.all_to_all(store, "z", 0, 0, tiled=True)

    wide = width // 8
    wo = lax.dynamic_slice_in_dim(out_proj, group * width + z * wide, wide)
    w = jnp.dot(wo, proj_in, preferred_element_type=f32).astype(bf16)

    k_own, k_swap, k_across, k_both, q_own, q_swap, q_across, q_both = prepare(
        after(queries, w)[0], keys[0], values[0], group
    )
    q_both = lax.ppermute(q_both, "core", SWAP)
    k_parts = [k_own, quad(k_swap, 1), quad(k_across, 2), quad(k_both, 3)]
    w_sum = butterfly(w, "yl", SWAP)
    q_hop = hop_y(after(q_both, w_sum), -1)
    w_sum = butterfly(w_sum, "x", NEAR)
    kv = jnp.concatenate(after(k_parts, w_sum), axis=0)
    q_parts = [q_own, quad(q_swap, 1), quad(after(q_across, q_hop), 2), hop_y(q_hop, -1)]

    w = w_sum = butterfly(w_sum, "x", FAR)
    w = lax.all_gather(w, "z", axis=0, tiled=True)

    clips = residual_in.shape[0]
    residual_in = after(residual_in, w_sum)
    res = jnp.dot(
        residual_in.reshape(clips * rows, residual_in.shape[2]), proj_in, preferred_element_type=f32
    ).astype(bf16)


    res = after(res, q_parts)
    res = lax.all_to_all(res.reshape(clips, rows, res.shape[1]), DP, 0, 0, tiled=True)

    readers = reader_map[0, :, 0]
    onehot = (readers[:, None] == jnp.arange(32, dtype=jnp.int32)[None, :]).astype(jnp.int32)
    before = jnp.cumsum(onehot, axis=0) - onehot
    rank = jnp.sum(before * onehot, axis=1)
    slot = ((readers % 4) ^ group) * 64 + (readers // 4) * 8 + rank
    pick = slot[:, None] == jnp.arange(256, dtype=jnp.int32)[None, :]

    stretch = stretch_ids[0]
    own = lax.dynamic_slice_in_dim(stretch, z * tokens, tokens)
    counts = jnp.sum((stretch[:, None] <= own[None, :]).astype(jnp.int32), axis=0)
    meta = jnp.stack([z, counts[0], counts[-1], group * rows])
    counts = counts.reshape(4, rows)
    counts = jnp.concatenate(
        [
            lax.dynamic_slice_in_dim(counts, i, 1)
            for i in (group, group ^ 1, group ^ 2, group ^ 3)
        ],
        axis=1,
    )
    def ring(pieces, *before):
        return [shift(after(v, before), k) for v, k in zip(pieces, (1, -1))]

    half = tokens // 2
    first = ring((kv, kv), store, w_sum, q_hop)
    second = ring(first, slot)
    *state, q_t = flash(q_parts, counts, meta, [kv] + first, [(0, 0), (1, 0), (2, 0)], (0, 7, 1), None, False)
    third = ring(second)
    state = flash(q_t, counts, meta, second, [(0, 0), (1, 0)], (6, 2), state, False)
    fourth = ring((third[0][:half], third[1][half:]))
    state = flash(q_t, counts, meta, third, [(0, 0), (1, 0)], (5, 3), state, False)
    att = flash(q_t, counts, meta, fourth, [(0, 0), (0, half)], (4,), state, True)

    features = store.shape[3]
    held = after(store, second)
    arrived = [
        lax.dynamic_index_in_dim(held, group ^ k, 1, keepdims=False).reshape(64, features) for k in range(4)
    ]
    arrived = jnp.concatenate(arrived[:1] + [quad(arrived[k], k) for k in range(1, 4)], axis=0)
    target = jnp.dot(pick.astype(bf16), arrived, preferred_element_type=f32)

    att = after(att, arrived)
    away = jnp.dot(att[: 2 * rows], w, preferred_element_type=f32).astype(bf16)
    away = lax.ppermute(away, "core", SWAP)
    part = jnp.dot(att[2 * rows :], w, preferred_element_type=f32) + away.astype(f32)
    partner = part[rows:].astype(bf16)
    half = rows // 2
    partner = jnp.concatenate([quad(partner[:half], 2), relay(partner[half:], -1)], axis=0)
    pre = part[:rows] + partner.astype(f32) + jnp.sum(res.astype(f32), axis=0)
    act = jax.nn.silu(pre).astype(bf16)
    projected = jnp.dot(act, proj_out, preferred_element_type=f32)
    cosine, grad_rows = align(projected, target)
    delta = grad_rows.astype(bf16)

    at = jnp.arange(512, dtype=jnp.int32)
    column = (
        (at // 4 % 8) * 128 + (at // 256) * 64 + (at // 64 % 4) * 8 + (at // 32 % 2) * 4 + at % 4
    )

    def chosen(c):
        take = (column + c * 32)[:, None] == jnp.arange(1024, dtype=jnp.int32)[None, :]
        return lax.dot_general(
            take.astype(bf16), act, (((1,), (1,)), ((), ())), preferred_element_type=f32
        ).astype(bf16)

    other_act = lax.ppermute(chosen(1 - core), "core", SWAP)
    other_delta = lax.ppermute(delta, "core", SWAP)
    grads = jnp.dot(
        jnp.concatenate([chosen(core), other_act], axis=1),
        jnp.concatenate([delta, other_delta], axis=0),
        preferred_element_type=f32,
    )
    grads = grads.astype(bf16).reshape(16, 32, grads.shape[1])
    grads = lax.all_to_all(grads, ("yh", "x", "yl"), 0, 0, tiled=True)
    grads = jnp.sum(grads.astype(f32), axis=0).astype(bf16).reshape(8, 4, grads.shape[2])
    grads = jnp.sum(lax.all_to_all(grads, "z", 0, 0, tiled=True).astype(f32), axis=0)
    return (cosine.reshape(1, rows), grads)


def solution(mesh):
    fine = Mesh(mesh.devices.reshape(SIZES), AXES)
    return jax.shard_map(
        on_device,
        mesh=fine,
        in_specs=(
            P(DP, SEQ, None),
            P(DP, SEQ, None),
            P(DP, SEQ, None),
            P(DP, None),
            P(None, SEQ, DP),
            P(None, DP),
            P(DP, None),
            P(),
            P(DP, SEQ, None, None),
            P(DP, SEQ, None),
        ),
        out_specs=(P(DP, SEQ), P(SEQ + DP, None)),
        check_vma=False,
    )
```

```python
import functools

import jax
import jax.numpy as jnp
from jax import lax
from jax.experimental import pallas as pl
from jax.experimental.pallas import tpu as pltpu
from jax.sharding import Mesh, PartitionSpec as P

HD = 128
HEADS = 24
GROUPS = 4
PER = HEADS // GROUPS
HEADS_STEP = 3
NEG = -1e30
EPS = 1e-06
SCALE2 = HD ** (-0.5) * 1.4426950408889634

AXES = ("z", "yh", "core", "x", "yl")
SIZES = (8, 2, 2, 4, 2)
SEQ = ("z", "yh", "core")
DP = ("x", "yl")
QUAD = ("yh", "core")
SWAP = ((0, 1), (1, 0))
NEAR = ((0, 1), (1, 0), (2, 3), (3, 2))
FAR = ((0, 3), (3, 0), (1, 2), (2, 1))


def flash_kernel(cuts, shifts, first, last, meta, *refs):
    if first:
        parts, refs = refs[:4], refs[4:]
    else:
        q_ref, refs = refs[0], refs[1:]
    n = len(cuts)
    c_ref, kv, refs = refs[0], refs[1 : 1 + n], refs[1 + n :]
    if not first:
        m_in, l_in, a_in = refs[:3]
        refs = refs[3:]
    if last:
        out, m_ref, l_ref, a_ref, qq, kk, vt = refs
    else:
        m_ref, l_ref, a_ref = refs[:3]
        qq, kk, vt = refs[-3:]
        if first:
            q_ref = refs[3]
    chunks = kk.shape[0]
    tokens = kk.shape[1]

    @pl.when(pl.program_id(0) == 0)
    def _():
        for piece, (j, row) in zip(kv, cuts):
            span = slice(row, row + piece.shape[0])
            kk[j, span, :HD] = piece[:, :HD]
            kk[j, span, HD:] = piece[:, :HD]
            vt[j, :HD, span] = piece[:, HD:].T
        vt[:, HD:, :] = jnp.ones((chunks, vt.shape[1] - HD, tokens), vt.dtype)

    if first:
        for i, part in enumerate(parts):
            rows = part.shape[0]
            for h in range(HEADS_STEP):
                q_ref[0, :, h * tokens + i * rows : h * tokens + (i + 1) * rows] = part[:, h * HD : (h + 1) * HD].T
        m_ref[...] = jnp.full(m_ref.shape, NEG, jnp.float32)
        l_ref[...] = jnp.zeros(l_ref.shape, jnp.float32)
        a_ref[...] = jnp.zeros(a_ref.shape, jnp.float32)
    else:
        m_ref[...] = m_in[...]
        l_ref[...] = l_in[...]
        a_ref[...] = a_in[...]
    scaled = q_ref[0].astype(jnp.float32) * SCALE2
    high = scaled.astype(jnp.bfloat16)
    qq[:HD] = high
    qq[HD:] = (scaled - high.astype(jnp.float32)).astype(jnp.bfloat16)

    def chunk(j, carry):
        far = shifts[0]
        for i in range(1, chunks):
            far = jnp.where(j == i, shifts[i], far)
        base = lax.rem(meta[0] + far, 8) * tokens

        def step(masked):
            s = jnp.dot(kk[j], qq[...], preferred_element_type=jnp.float32)
            if masked:
                place = lax.broadcasted_iota(jnp.int32, s.shape, 0) ^ meta[3]
                s = jnp.where(place < c_ref[...] - base, s, NEG)
            old = m_ref[0]
            new = jnp.maximum(old, jnp.max(s, axis=0, keepdims=True))
            p = jnp.exp2(s - new).astype(jnp.bfloat16)
            factor = jnp.exp2(old - new)
            sums = jnp.dot(vt[j], p, preferred_element_type=jnp.float32)
            m_ref[0] = new
            l_ref[0] = l_ref[0] * factor + sums[HD : HD + 1]
            a_ref[0] = a_ref[0] * factor + sums[:HD]

        whole = base + tokens <= meta[1]

        @pl.when(whole)
        def _():
            step(False)

        @pl.when(jnp.logical_and(jnp.logical_not(whole), base < meta[2]))
        def _():
            step(True)

        return carry

    lax.fori_loop(0, chunks, chunk, 0)
    if last:
        done = (a_ref[0] / l_ref[0]).astype(out.dtype)
        rows = tokens // 4
        for h in range(HEADS_STEP):
            for to, block in enumerate((1, 3, 0, 2)):
                start = h * tokens + block * rows
                out[to * rows : (to + 1) * rows, h * HD : (h + 1) * HD] = done[:, start : start + rows].T


def flash(q_t, counts, meta, pieces, cuts, shifts, state, last):
    first = state is None
    tokens = counts.shape[1]
    wide = HEADS_STEP * tokens
    steps = PER // HEADS_STEP
    chunks = len(shifts)
    f32, bf16 = jnp.float32, jnp.bfloat16
    row = pl.BlockSpec((1, 1, wide), lambda h, meta: (h, 0, 0))
    head = pl.BlockSpec((1, HD, wide), lambda h, meta: (h, 0, 0))
    if first:
        in_specs = [pl.BlockSpec((tokens // 4, HEADS_STEP * HD), lambda h, meta: (0, h))] * 4
        args = list(q_t)
    else:
        in_specs = [head]
        args = [q_t]
    in_specs += [pl.BlockSpec((1, wide), lambda h, meta: (0, 0))]
    in_specs += [pl.BlockSpec(p.shape, lambda h, meta: (0, 0)) for p in pieces]
    args += [jnp.concatenate([counts] * HEADS_STEP, axis=1)] + list(pieces)
    if not first:
        in_specs += [row, row, head]
        args += list(state)
    scratch = [
        pltpu.VMEM((2 * HD, wide), bf16),
        pltpu.VMEM((chunks, tokens, 2 * HD), bf16),
        pltpu.VMEM((chunks, HD + 16, tokens), bf16),
    ]
    if last:
        out_specs = pl.BlockSpec((tokens, HEADS_STEP * HD), lambda h, meta: (0, h))
        out_shape = jax.ShapeDtypeStruct((tokens, PER * HD), bf16)
        scratch = [
            pltpu.VMEM((1, 1, wide), f32),
            pltpu.VMEM((1, 1, wide), f32),
            pltpu.VMEM((1, HD, wide), f32),
        ] + scratch
    else:
        out_specs = [row, row, head]
        out_shape = [
            jax.ShapeDtypeStruct((steps, 1, wide), f32),
            jax.ShapeDtypeStruct((steps, 1, wide), f32),
            jax.ShapeDtypeStruct((steps, HD, wide), f32),
        ]
        if first:
            out_specs.append(head)
            out_shape.append(jax.ShapeDtypeStruct((steps, HD, wide), bf16))
    return pl.pallas_call(
        functools.partial(flash_kernel, tuple(cuts), tuple(shifts), first, last),
        grid_spec=pltpu.PrefetchScalarGridSpec(
            num_scalar_prefetch=1,
            grid=(steps,),
            in_specs=in_specs,
            out_specs=out_specs,
            scratch_shapes=scratch,
        ),
        out_shape=out_shape,
        compiler_params=pltpu.CompilerParams(vmem_limit_bytes=48 * 1024 * 1024),
        cost_estimate=pl.CostEstimate(
            flops=40 * PER * tokens * tokens * chunks * HD,
            bytes_accessed=10 * PER * HD * tokens,
            transcendentals=PER * tokens * tokens * chunks,
        ),
    )(meta, *args)


def prepare_kernel(
    meta, q_ref, k_ref, v_ref, kv_own, kv_swap, kv_across, kv_both, q_own, q_swap, q_across, q_both
):
    width = PER * HD

    def take(g, kv, q):
        k = k_ref[:, pl.ds(pl.multiple_of(g * HD, HD), HD)]
        v = v_ref[:, pl.ds(pl.multiple_of(g * HD, HD), HD)]
        kv[...] = jnp.concatenate([k, v], axis=1)
        q[...] = q_ref[:, pl.ds(pl.multiple_of(g * width, HD), width)]

    group = meta[0]
    take(group, kv_own, q_own)
    take(group ^ 1, kv_swap, q_swap)
    take(group ^ 2, kv_across, q_across)
    take(group ^ 3, kv_both, q_both)


def prepare(queries, keys, values, group):
    rows = queries.shape[0]
    shapes = [(rows, w) for w in (2 * HD, PER * HD) for _ in range(4)]
    return pl.pallas_call(
        prepare_kernel,
        grid=(1,),
        in_specs=[pl.BlockSpec(memory_space=pltpu.SMEM)]
        + [pl.BlockSpec(a.shape, lambda i: (0, 0)) for a in (queries, keys, values)],
        out_specs=[pl.BlockSpec(s, lambda i: (0, 0)) for s in shapes],
        out_shape=[jax.ShapeDtypeStruct(s, jnp.bfloat16) for s in shapes],
        compiler_params=pltpu.CompilerParams(vmem_limit_bytes=60 * 1024 * 1024),
    )(group[None].astype(jnp.int32), queries, keys, values)


def shift(v, k):
    return lax.ppermute(v, "z", [(i, (i + k) % 8) for i in range(8)])


def hop_y(v, k):
    return lax.ppermute(v, ("yh", "yl"), [(i, (i + k) % 4) for i in range(4)])


def relay(v, k):
    return hop_y(hop_y(v, k), k)


def butterfly(v, axis, pairs):
    return (v.astype(jnp.float32) + lax.ppermute(v, axis, pairs).astype(jnp.float32)).astype(v.dtype)


def quad(v, k):
    return lax.ppermute(v, QUAD, [(i, i ^ k) for i in range(4)])


def after(v, other):
    return lax.optimization_barrier((v, other))[0]


def align(projected, target):
    proj_square = jnp.sum(projected * projected, axis=-1) + EPS
    target_square = jnp.sum(target * target, axis=-1) + EPS
    inner = jnp.sum(projected * target, axis=-1)
    denominator = jnp.sqrt(proj_square * target_square)
    cosine = inner / denominator
    grad_rows = -(target / denominator[:, None] - (cosine / proj_square)[:, None] * projected)
    return (cosine, grad_rows)


def on_device(
    queries,
    keys,
    values,
    stretch_ids,
    residual_in,
    out_proj,
    proj_in,
    proj_out,
    teacher_store,
    reader_map,
):
    f32, bf16 = jnp.float32, jnp.bfloat16
    z = lax.axis_index("z")
    yh = lax.axis_index("yh")
    core = lax.axis_index("core")
    group = yh * 2 + core
    rows = queries.shape[1]
    tokens = rows * 4
    width = PER * HD

    store = teacher_store.reshape(8, 4, 8, teacher_store.shape[3])
    store = lax.all_to_all(store, "z", 0, 0, tiled=True)

    wide = width // 8
    wo = lax.dynamic_slice_in_dim(out_proj, group * width + z * wide, wide)
    w = jnp.dot(wo, proj_in, preferred_element_type=f32).astype(bf16)

    k_own, k_swap, k_across, k_both, q_own, q_swap, q_across, q_both = prepare(
        after(queries, w)[0], keys[0], values[0], group
    )
    q_both = lax.ppermute(q_both, "core", SWAP)
    k_parts = [k_own, quad(k_swap, 1), quad(k_across, 2), quad(k_both, 3)]
    w_sum = butterfly(w, "yl", SWAP)
    q_hop = hop_y(after(q_both, w_sum), -1)
    w_sum = butterfly(w_sum, "x", NEAR)
    kv = jnp.concatenate(after(k_parts, w_sum), axis=0)
    q_parts = [q_own, quad(q_swap, 1), quad(after(q_across, q_hop), 2), hop_y(q_hop, -1)]

    w = w_sum = butterfly(w_sum, "x", FAR)
    w = lax.all_gather(w, "z", axis=0, tiled=True)

    clips = residual_in.shape[0]
    residual_in = after(residual_in, w_sum)
    res = jnp.dot(
        residual_in.reshape(clips * rows, residual_in.shape[2]), proj_in, preferred_element_type=f32
    ).astype(bf16)


    res = after(res, q_parts)
    res = lax.all_to_all(res.reshape(clips, rows, res.shape[1]), DP, 0, 0, tiled=True)

    readers = reader_map[0, :, 0]
    onehot = (readers[:, None] == jnp.arange(32, dtype=jnp.int32)[None, :]).astype(jnp.int32)
    before = jnp.cumsum(onehot, axis=0) - onehot
    rank = jnp.sum(before * onehot, axis=1)
    slot = ((readers % 4) ^ group) * 64 + (readers // 4) * 8 + rank
    pick = slot[:, None] == jnp.arange(256, dtype=jnp.int32)[None, :]

    stretch = stretch_ids[0]
    own = lax.dynamic_slice_in_dim(stretch, z * tokens, tokens)
    counts = jnp.sum((stretch[:, None] <= own[None, :]).astype(jnp.int32), axis=0)
    meta = jnp.stack([z, counts[0], counts[-1], group * rows])
    counts = counts.reshape(4, rows)
    counts = jnp.concatenate(
        [
            lax.dynamic_slice_in_dim(counts, i, 1)
            for i in (group, group ^ 1, group ^ 2, group ^ 3)
        ],
        axis=1,
    )
    def ring(pieces, *before):
        return [shift(after(v, before), k) for v, k in zip(pieces, (1, -1))]

    half = tokens // 2
    first = ring((kv, kv), store, w_sum, q_hop)
    second = ring(first, slot)
    *state, q_t = flash(q_parts, counts, meta, [kv] + first, [(0, 0), (1, 0), (2, 0)], (0, 7, 1), None, False)
    third = ring(second)
    state = flash(q_t, counts, meta, second, [(0, 0), (1, 0)], (6, 2), state, False)
    fourth = ring((third[0][:half], third[1][half:]))
    state = flash(q_t, counts, meta, third, [(0, 0), (1, 0)], (5, 3), state, False)
    att = flash(q_t, counts, meta, fourth, [(0, 0), (0, half)], (4,), state, True)

    features = store.shape[3]
    held = after(store, second)
    arrived = [
        lax.dynamic_index_in_dim(held, group ^ k, 1, keepdims=False).reshape(64, features) for k in range(4)
    ]
    arrived = jnp.concatenate(arrived[:1] + [quad(arrived[k], k) for k in range(1, 4)], axis=0)
    att, arrived = lax.optimization_barrier((att, arrived))
    target = jnp.dot(pick.astype(bf16), arrived, preferred_element_type=f32)

    away = jnp.dot(att[: 2 * rows], w, preferred_element_type=f32).astype(bf16)
    away = lax.ppermute(away, "core", SWAP)
    part = jnp.dot(att[2 * rows :], w, preferred_element_type=f32) + away.astype(f32)
    partner = part[rows:].astype(bf16)
    half = rows // 2
    partner = jnp.concatenate([quad(partner[:half], 2), relay(partner[half:], -1)], axis=0)
    pre = part[:rows] + partner.astype(f32) + jnp.sum(res.astype(f32), axis=0)
    act = jax.nn.silu(pre).astype(bf16)
    projected = jnp.dot(act, proj_out, preferred_element_type=f32)
    cosine, grad_rows = align(projected, target)
    delta = grad_rows.astype(bf16)

    at = jnp.arange(512, dtype=jnp.int32)
    column = (
        (at // 4 % 8) * 128 + (at // 256) * 64 + (at // 64 % 4) * 8 + (at // 32 % 2) * 4 + at % 4
    )

    def chosen(c):
        take = (column + c * 32)[:, None] == jnp.arange(1024, dtype=jnp.int32)[None, :]
        return lax.dot_general(
            take.astype(bf16), act, (((1,), (1,)), ((), ())), preferred_element_type=f32
        ).astype(bf16)

    other_act = lax.ppermute(chosen(1 - core), "core", SWAP)
    other_delta = lax.ppermute(delta, "core", SWAP)
    grads = jnp.dot(
        jnp.concatenate([chosen(core), other_act], axis=1),
        jnp.concatenate([delta, other_delta], axis=0),
        preferred_element_type=f32,
    )
    grads = grads.astype(bf16).reshape(16, 32, grads.shape[1])
    grads = lax.all_to_all(grads, ("yh", "x", "yl"), 0, 0, tiled=True)
    grads = jnp.sum(grads.astype(f32), axis=0).astype(bf16).reshape(8, 4, grads.shape[2])
    grads = jnp.sum(lax.all_to_all(grads, "z", 0, 0, tiled=True).astype(f32), axis=0)
    return (cosine.reshape(1, rows), grads)


def solution(mesh):
    fine = Mesh(mesh.devices.reshape(SIZES), AXES)
    return jax.shard_map(
        on_device,
        mesh=fine,
        in_specs=(
            P(DP, SEQ, None),
            P(DP, SEQ, None),
            P(DP, SEQ, None),
            P(DP, None),
            P(None, SEQ, DP),
            P(None, DP),
            P(DP, None),
            P(),
            P(DP, SEQ, None, None),
            P(DP, SEQ, None),
        ),
        out_specs=(P(DP, SEQ), P(SEQ + DP, None)),
        check_vma=False,
    )
```
